1024 devices in a mesh: dp: 16 (over y, core), expert: 64 (over z, x).
Axes of the slice: x: 4, y: 8, z: 16, core: 2. Of those that a mesh axis runs over, the one named last changes fastest.
Arguments:
- grad_out: bfloat16 [131072, 2048], P(('dp', 'expert')), may hold values from -6 to 6
- route_prob: bfloat16 [131072, 1], P(('dp', 'expert')), may hold values from 0.099609375 to 1
- expert_ids: int32 [131072, 1], P(('dp', 'expert')), may hold values from 0 to 63; in each aligned block of 128 rows (0 to 127, 128 to 255, ...) at most 3 rows name the same one
- saved_act: bfloat16 [16, 64, 192, 768], P('dp', 'expert'), may hold values from -0.21875 to 0.21875
- down_weight: bfloat16 [64, 768, 2048], P('expert'), may hold values from -0.21875 to 0.21875
Outputs:
- grad_act: bfloat16 [16, 64, 192, 768], P('dp', 'expert')
- grad_weight: float32 [64, 2048, 768], P('expert', 'dp')
- grad_prob: float32 [131072, 1], P(('dp', 'expert'))
The draws below stay inside these ranges and needn't reach their ends.
Inputs may be any that keep to these rules, and one draw needn't show every extreme that they name: `expert_ids`: among the 128 tokens of one device no expert is named more than 3 times, a bound that some block reaches on every device.
All inputs are finite; a program needn't handle non-finite values.
Results may differ from the reference program's by a relative error of at most 0.0029.
Values may be sent and summed in bfloat16 or wider, within the bound.
A program may use at most 32 MiB of HBM per device.

```python
import math
import jax
import jax.numpy as jnp
import numpy as np
from jax import lax

D = 2048
FFW = 768
ROUTED = 1
TOK_DEV = 128
EXPERTS = 64
CAP = 3
SLOTS = 192
TOKENS = 131072
N_DP = 16
N_EXPERT = 64


def steps_of(stream_key, shape, cuts, smallest, top_value):
    def one(axis_at, parts):
        heights = jax.random.uniform(jax.random.fold_in(jax.random.fold_in(stream_key, 6), axis_at), (parts,), jnp.float32, smallest / len(cuts), top_value / len(cuts))
        return jnp.repeat(jnp.exp(heights), shape[axis_at] // parts).reshape((-1,) + (1,) * (len(shape) - axis_at - 1))

    factor_of = one(*cuts[0])
    for cut in cuts[1:]:
        factor_of = factor_of * one(*cut)
    return factor_of


def routed_block(stream_key, own, number, rows, number_of, top, reach, skew):
    order = jax.random.permutation(stream_key, number_of)
    packed, ordinary = shares(number_of, rows * top, reach, skew, True), shares(number_of, rows * top, reach, skew, False)
    places = jnp.arange(number_of)

    def named(sizes, turn):
        used = int((sizes > 0).sum())
        fixed = max(1, used // 4)
        passed = fixed + (places - fixed + turn * (used - fixed)) % max(1, number_of - fixed)
        return jnp.zeros((number_of,), jnp.int32).at[order[jnp.where(places < fixed, places, passed)]].set(jnp.asarray(sizes, jnp.int32))

    sizes = jnp.where(number % 4 == 0, named(packed, number // 4), named(ordinary, number - number // 4 - 1))
    mixed = jax.random.permutation(jax.random.fold_in(own, 3), number_of)
    source_of, receiver = mixed[0:number_of // 2 * 2:2], mixed[1:number_of // 2 * 2:2]
    slack = jnp.minimum(sizes[source_of] - 1, reach - sizes[receiver]) // 2
    slack = jnp.where((source_of == order[0]) | (receiver == order[0]) | (sizes[receiver] == 0), 0, jnp.maximum(slack, 0))
    passed = jax.random.randint(jax.random.fold_in(own, 4), (number_of // 2,), 0, 1 << 20) % (slack + 1)
    sizes = sizes.at[source_of].add(-passed).at[receiver].add(passed)
    members = jnp.searchsorted(jnp.cumsum(sizes), jnp.arange(rows * top), side="right").astype(jnp.int32)
    grid = members.reshape(top, rows).T
    grid = grid[jax.random.permutation(jax.random.fold_in(own, 1), rows)]
    turn = jax.random.randint(jax.random.fold_in(own, 2), (rows, 1), 0, top)
    return jnp.take_along_axis(grid, (jnp.arange(top)[None, :] + turn) % top, axis=1)


def shares(count, total, limit, skew, full):
    portions = [(1 << 20) // math.isqrt(standing ** skew) + 1 for standing in range(1, count + 1)]
    largest = limit if full else min(limit, max(-(-total // count), total * portions[0] // sum(portions)))
    least = 1 if total - largest >= count - 1 else 0
    counts, surplus = [largest] + [least] * (count - 1), total - largest - least * (count - 1)
    while surplus > 0:
        movable = [i for i in range(1, count) if counts[i] < largest] or [i for i in range(1, count) if counts[i] < limit]
        whole, budget = sum([portions[i] for i in movable]), surplus
        for i in movable:
            extra = min(limit - counts[i], max(1, budget * portions[i] // whole), surplus)
            counts[i] = counts[i] + extra
            surplus = surplus - extra
    return np.array(counts)


def noise(rng, shape, width, reach, shards=(), kind=jnp.bfloat16):
    result = jax.random.normal(rng, shape, jnp.float32) * width
    if len(shards) > 0:
        result = steps_of(rng, shape, shards, -0.22, 0.18) * result
    return jnp.clip(result, min=-reach, max=reach).astype(kind)


def setup_inputs(seed: int = 0) -> dict:
    streams_of = jax.random.split(jax.random.key(seed), 6)
    grad_out = noise(streams_of[0], (TOKENS, D), 1.0, 6.0, ((0, 1024),))
    route_prob = jnp.clip(0.099609375 + 0.9003906 * jax.random.uniform(streams_of[1], (TOKENS, ROUTED), jnp.float32) ** steps_of(streams_of[1], (TOKENS, ROUTED), ((0, 1024),), -0.2, 0.2), 0.099609375, 1.0).astype(jnp.bfloat16)
    expert_ids_keys = jax.random.split(jax.random.fold_in(streams_of[2], 1), TOKENS // TOK_DEV)
    expert_ids_turns = jax.random.permutation(jax.random.fold_in(streams_of[2], 3), TOKENS // TOK_DEV)
    expert_ids = jax.vmap(lambda own, number: routed_block(jax.random.fold_in(streams_of[2], 2), own, number, TOK_DEV, EXPERTS, 1, CAP, 2))(expert_ids_keys, expert_ids_turns).reshape((TOKENS, ROUTED))
    saved_act = noise(streams_of[3], (N_DP, EXPERTS, SLOTS, FFW), (FFW ** -0.5), 0.21875, ((0, 16), (1, 64)))
    down_weight = noise(streams_of[4], (EXPERTS, FFW, D), FFW ** -0.5, 0.21875, ((0, 64),))
    return {"grad_out": grad_out, "route_prob": route_prob, "expert_ids": expert_ids, "saved_act": saved_act, "down_weight": down_weight}


def reference(grad_out, route_prob, expert_ids, saved_act, down_weight):
    groups = N_DP * N_EXPERT
    routed = expert_ids[:, 0].reshape(groups, TOK_DEV)
    member = (routed[:, :, None] == jnp.arange(EXPERTS, dtype=jnp.int32)[None, None, :]).astype(jnp.int32)
    before = jnp.cumsum(member, axis=1) - member
    within = jnp.sum(before * member, axis=2)
    device = jnp.arange(groups, dtype=jnp.int32)[:, None]
    source = device % N_EXPERT
    replica = device // N_EXPERT
    position = source * CAP + within
    flat_index = ((replica * EXPERTS + routed) * SLOTS + position).reshape(-1).astype(jnp.int32)
    token_index = jnp.arange(TOKENS, dtype=jnp.int32)
    lookup = jnp.full((N_DP * EXPERTS * SLOTS,), TOKENS, jnp.int32).at[flat_index].set(token_index)
    lookup = lookup.reshape(N_DP, EXPERTS, SLOTS)
    prob_column = route_prob[:, 0]

    def one_expert(expert):
        chosen = lookup[:, expert]
        arrived = jnp.take(grad_out, chosen, axis=0, mode="fill", fill_value=0).astype(jnp.float32)
        arrived_prob = jnp.take(prob_column, chosen, axis=0, mode="fill", fill_value=0).astype(jnp.float32)[..., None]
        stored = saved_act[:, expert].astype(jnp.float32)
        weight = down_weight[expert].astype(jnp.float32)
        backed = jnp.einsum("rsd,fd->rsf", arrived, weight)
        grad_act = (arrived_prob * backed).astype(jnp.bfloat16)
        slot_grad = jnp.sum(backed * stored, axis=2)
        weighted = lax.optimization_barrier((arrived_prob * arrived).astype(jnp.bfloat16)).astype(jnp.float32)
        partial_value = jnp.einsum("rsd,rsf->rdf", weighted, stored)
        return grad_act, jnp.sum(partial_value, axis=0), slot_grad

    grad_act, grad_weight, slot_grad = lax.map(one_expert, jnp.arange(EXPERTS, dtype=jnp.int32))
    grad_act = jnp.transpose(grad_act, (1, 0, 2, 3))
    slot_flat = jnp.transpose(slot_grad, (1, 0, 2)).reshape(-1)
    grad_prob = slot_flat[flat_index][:, None]
    return grad_act, grad_weight, grad_prob
```

```python
import functools

import jax
import jax.numpy as jnp
from jax import lax
from jax.experimental import pallas as pl
from jax.experimental.pallas import tpu as pltpu
from jax.sharding import PartitionSpec as P

MESH = pl.DeviceIdType.MESH
NZ, NX = 16, 4
NE = NZ * NX
NDP = 16
CAP = 3
CHUNKS = 4
PEERS = NE // CHUNKS
ROWS = PEERS * CAP
SLOTS = NE * CAP
SELF = NE - NX
TOK = 128
WIDTH = 2048
FFW = 768
PIECES = WIDTH // 128
F32 = jnp.float32
BF16 = jnp.bfloat16


def offset_of(o):
    q = o // NX
    half = (q + 1) // 2
    return NZ // 2 + half * (1 - 2 * (q % 2)), o % NX


def target_of(o, z, x):
    dz, dx = offset_of(o)
    return ((z + dz) % NZ) * NX + (x + dx) % NX


def source_of(o, z, x):
    dz, dx = offset_of(o)
    return ((z + NZ - dz) % NZ) * NX + (x + NX - dx) % NX


def slot_parts(slot):
    chunk = (
        (slot >= ROWS).astype(jnp.int32)
        + (slot >= 2 * ROWS).astype(jnp.int32)
        + (slot >= 3 * ROWS).astype(jnp.int32)
    )
    rest = slot - ROWS * chunk
    return PEERS * chunk + rest % PEERS, rest // PEERS


def dot(a, b):
    return lax.dot_general(a, b, (((1,), (0,)), ((), ())), preferred_element_type=F32)


def kernel(
    ids_ref, prob_ref, grad_hbm, saved_hbm, weight_hbm,
    act_ref, gw_ref, gp_ref,
    grad, saved, weight, onehot, swap, to_natural,
    send, recv, psend, precv, gsend, grecv,
    arrived, act, wsend, wrecv, gathered,
    load_sem, tok_send, tok_recv, p_send, p_recv, g_send, g_recv,
    w_send, w_recv, s_send, right_recv, left_recv, twin_recv,
):
    dp, me = lax.axis_index("dp"), lax.axis_index("expert")
    z, x = me // NX, me % NX
    y, core = dp // 2, dp % 2
    twin = dp + 1 - 2 * core
    right, left = (dp + 2) % NDP, (dp + NDP - 2) % NDP

    barrier = pltpu.get_barrier_semaphore()

    @pl.loop(0, NE)
    def _(o):
        @pl.when(o != SELF)
        def _():
            pl.semaphore_signal(
                barrier, inc=1, device_id=(dp, target_of(o, z, x)), device_id_type=MESH
            )

    @pl.loop(1, NDP)
    def _(i):
        pl.semaphore_signal(
            barrier, inc=1, device_id=((dp + i) % NDP, me), device_id_type=MESH
        )

    loads = [
        pltpu.make_async_copy(grad_hbm, grad, load_sem.at[0]),
        pltpu.make_async_copy(saved_hbm, saved, load_sem.at[1]),
        pltpu.make_async_copy(weight_hbm, weight, load_sem.at[2]),
    ]
    for load in loads:
        load.start()

    ids = jnp.broadcast_to(ids_ref[...], (TOK, TOK)).astype(F32)
    earlier = lax.broadcasted_iota(jnp.int32, (TOK, TOK), 0) < lax.broadcasted_iota(
        jnp.int32, (TOK, TOK), 1
    )
    same = jnp.where(earlier & (ids.T == ids), 1.0, 0.0)
    before = jnp.sum(same, axis=0, keepdims=True)
    peer, k = slot_parts(lax.broadcasted_iota(jnp.int32, (SLOTS, TOK), 0))
    onehot[...] = jnp.where(
        (target_of(peer, z, x) == ids_ref[...]) & (k.astype(F32) == before), 1.0, 0.0
    )
    lane = lax.broadcasted_iota(jnp.int32, (PEERS, 128), 1)

    def by_lane(column):
        out = jnp.zeros((PEERS, 128), F32)
        for i in range(CAP):
            out = jnp.where(lane == i, column[PEERS * i : PEERS * (i + 1)], out)
        return out

    probs = jnp.sum(onehot[...] * prob_ref[...].astype(F32), axis=1, keepdims=True)
    for j in range(CHUNKS):
        psend[PEERS * j : PEERS * (j + 1), 0, :] = by_lane(probs[ROWS * j : ROWS * (j + 1)])

    row = lax.broadcasted_iota(jnp.int32, (256, 256), 0)
    col = lax.broadcasted_iota(jnp.int32, (256, 256), 1)
    swap[...] = jnp.where(col == 16 * (row % 16) + row // 16, 1.0, 0.0).astype(BF16)

    loads[0].wait()
    for j in range(CHUNKS):
        picked = dot(onehot[ROWS * j : ROWS * (j + 1), :].astype(BF16), grad[...]).astype(BF16)
        for i in range(CAP):
            tiles = jnp.concatenate(
                [picked[PEERS * i : PEERS * (i + 1), 128 * c : 128 * (c + 1)] for c in range(PIECES)],
                axis=0,
            )
            out = dot(swap[...], tiles).astype(BF16).reshape(PEERS, PIECES, 128)
            send[PEERS * j : PEERS * (j + 1), PIECES * i : PIECES * (i + 1), :] = out
        if j == 0:
            pl.semaphore_wait(barrier, NE - 1 + NDP - 1)

        @pl.loop(PEERS * j, min(PEERS * (j + 1), NE))
        def _(o):
            @pl.when(o != SELF)
            def _():
                peer_id = (dp, target_of(o, z, x))
                pltpu.make_async_remote_copy(
                    src_ref=send.at[o], dst_ref=recv.at[o],
                    send_sem=tok_send, recv_sem=tok_recv.at[j],
                    device_id=peer_id, device_id_type=MESH,
                ).start()
                pltpu.make_async_remote_copy(
                    src_ref=psend.at[o], dst_ref=precv.at[o],
                    send_sem=p_send, recv_sem=p_recv.at[j],
                    device_id=peer_id, device_id_type=MESH,
                ).start()

    recv[SELF] = send[SELF]
    precv[SELF] = psend[SELF]

    slot_r = lax.broadcasted_iota(jnp.int32, (SLOTS, SLOTS), 0)
    slot_c = lax.broadcasted_iota(jnp.int32, (SLOTS, SLOTS), 1)
    peer_r, k_r = slot_parts(slot_r)
    to_chunk = jnp.where(source_of(peer_r, z, x) * CAP + k_r == slot_c, 1.0, 0.0).astype(BF16)
    peer_c, k_c = slot_parts(slot_c)
    to_natural[...] = jnp.where(
        source_of(peer_c, z, x) * CAP + k_c == slot_r, 1.0, 0.0
    ).astype(BF16)
    loads[1].wait()
    own = dot(to_chunk, saved[...]).astype(BF16)
    for j in range(CHUNKS):
        gathered[j, dp] = own[ROWS * j : ROWS * (j + 1)]

    def pass_on(j, r, device, sem):
        pltpu.make_async_remote_copy(
            src_ref=gathered.at[j, r], dst_ref=gathered.at[j, r],
            send_sem=s_send, recv_sem=sem,
            device_id=(device, me), device_id_type=MESH,
        ).start()

    def await_piece(j, r, sem):
        pltpu.make_async_remote_copy(
            src_ref=gathered.at[j, r], dst_ref=gathered.at[j, r],
            send_sem=s_send, recv_sem=sem,
            device_id=(twin, me), device_id_type=MESH,
        ).wait_recv()

    for j in range(CHUNKS):
        pass_on(j, dp, right, right_recv.at[0, j])
        pass_on(j, dp, left, left_recv.at[0, j])
    for j in range(CHUNKS):
        pass_on(j, dp, twin, twin_recv)
    for hop in range(1, 5):
        from_left, from_right = (dp + NDP - 2 * hop) % NDP, (dp + 2 * hop) % NDP
        for j in range(CHUNKS):
            if hop < 4 or j < 2:
                await_piece(j, from_left, right_recv.at[hop - 1, j])
                if hop < 3 or (hop == 3 and j < 2):
                    pass_on(j, from_left, right, right_recv.at[hop, j])
                pass_on(j, from_left, twin, twin_recv)
            if hop < 4 or j >= 2:
                await_piece(j, from_right, left_recv.at[hop - 1, j])
                if hop < 3 or (hop == 3 and j >= 2):
                    pass_on(j, from_right, left, left_recv.at[hop, j])
                pass_on(j, from_right, twin, twin_recv)
    loads[2].wait()

    def take(j):
        count = PEERS - (1 if j == CHUNKS - 1 else 0)
        pltpu.make_async_remote_copy(
            src_ref=send.at[pl.ds(0, count)], dst_ref=recv.at[pl.ds(0, count)],
            send_sem=tok_send, recv_sem=tok_recv.at[j],
            device_id=(dp, me), device_id_type=MESH,
        ).wait_recv()
        pltpu.make_async_remote_copy(
            src_ref=psend.at[pl.ds(0, count)], dst_ref=precv.at[pl.ds(0, count)],
            send_sem=p_send, recv_sem=p_recv.at[j],
            device_id=(dp, me), device_id_type=MESH,
        ).wait_recv()
        factor = precv[PEERS * j : PEERS * (j + 1), 0, :]
        for i in range(CAP):
            tiles = recv[PEERS * j : PEERS * (j + 1), PIECES * i : PIECES * (i + 1), :]
            turned = dot(swap[...], tiles.reshape(PEERS * PIECES, 128))
            part = jnp.broadcast_to(factor[:, i : i + 1], (PEERS, 128))
            at = ROWS * j + PEERS * i
            for c in range(PIECES):
                tile = turned[PEERS * c : PEERS * (c + 1)]
                arrived[at : at + PEERS, 128 * c : 128 * (c + 1)] = tile.astype(BF16)
                wsend[j, c, PEERS * i : PEERS * (i + 1), :] = (tile * part).astype(BF16)
        wrecv[j, dp] = wsend[j, dp]

        @pl.loop(1, NDP)
        def _(i):
            to = (dp + i) % NDP
            pltpu.make_async_remote_copy(
                src_ref=wsend.at[j, to], dst_ref=wrecv.at[j, dp],
                send_sem=w_send, recv_sem=w_recv.at[j],
                device_id=(to, me), device_id_type=MESH,
            ).start()

    def back(j):
        rows = slice(ROWS * j, ROWS * (j + 1))
        backed = lax.dot_general(
            arrived[rows, :], weight[...], (((1,), (1,)), ((), ())), preferred_element_type=F32
        )
        mine = gathered[j, dp].astype(F32)
        gsend[PEERS * j : PEERS * (j + 1), 0, :] = by_lane(
            jnp.sum(backed * mine, axis=1, keepdims=True)
        )

        @pl.loop(PEERS * j, PEERS * (j + 1))
        def _(o):
            @pl.when(o != SELF)
            def _():
                pltpu.make_async_remote_copy(
                    src_ref=gsend.at[o], dst_ref=grecv.at[o],
                    send_sem=g_send, recv_sem=g_recv,
                    device_id=(dp, source_of(o, z, x)), device_id_type=MESH,
                ).start()

        factor = precv[PEERS * j : PEERS * (j + 1), 0, :]
        for i in range(CAP):
            part = jnp.broadcast_to(factor[:, i : i + 1], (PEERS, FFW))
            at = PEERS * i
            act[ROWS * j + at : ROWS * j + at + PEERS, :] = (
                part * backed[at : at + PEERS]
            ).astype(BF16)

    def add(j):
        pltpu.make_async_remote_copy(
            src_ref=wsend.at[j, pl.ds(0, NDP - 1)], dst_ref=wrecv.at[j, pl.ds(0, NDP - 1)],
            send_sem=w_send, recv_sem=w_recv.at[j],
            device_id=(dp, me), device_id_type=MESH,
        ).wait_recv()
        part = lax.dot_general(
            wrecv[j].reshape(NDP * ROWS, 128), gathered[j].reshape(NDP * ROWS, FFW),
            (((0,), (0,)), ((), ())), preferred_element_type=F32,
        )
        if j == 0:
            gw_ref[...] = part
        else:
            gw_ref[...] += part

    take(0)
    back(0)
    take(1)
    back(1)
    pltpu.make_async_remote_copy(
        src_ref=gathered.at[:, pl.ds(0, NDP // 2)], dst_ref=gathered.at[:, pl.ds(0, NDP // 2)],
        send_sem=s_send, recv_sem=twin_recv, device_id=(twin, me), device_id_type=MESH,
    ).wait_recv()
    take(2)
    take(3)
    back(2)
    back(3)
    grecv[SELF] = gsend[SELF]
    add(0)
    add(1)
    act_ref[...] = dot(to_natural[...], act[...]).astype(BF16)
    add(2)
    add(3)

    def all_but_one(ref, sem):
        return pltpu.make_async_remote_copy(
            src_ref=ref.at[pl.ds(0, NE - 1)], dst_ref=ref.at[pl.ds(0, NE - 1)],
            send_sem=sem, recv_sem=g_recv, device_id=(dp, me), device_id_type=MESH,
        )

    all_but_one(grecv, g_send).wait_recv()
    total = jnp.zeros((PEERS, TOK), F32)
    for j in range(CHUNKS):
        back_sum = grecv[PEERS * j : PEERS * (j + 1), 0, :]
        for i in range(CAP):
            at = ROWS * j + PEERS * i
            total += onehot[at : at + PEERS, :] * jnp.broadcast_to(
                back_sum[:, i : i + 1], (PEERS, TOK)
            )
    gp_ref[...] = jnp.sum(total, axis=0, keepdims=True)

    all_but_one(send, tok_send).wait_send()
    all_but_one(psend, p_send).wait_send()
    all_but_one(gsend, g_send).wait_send()
    pltpu.make_async_remote_copy(
        src_ref=wsend.at[:, pl.ds(0, NDP - 1)], dst_ref=wsend.at[:, pl.ds(0, NDP - 1)],
        send_sem=w_send, recv_sem=g_recv, device_id=(dp, me), device_id_type=MESH,
    ).wait_send()
    pltpu.make_async_remote_copy(
        src_ref=gathered.at[:, pl.ds(0, NDP - 1)], dst_ref=gathered.at[:, pl.ds(0, NDP - 1)],
        send_sem=s_send, recv_sem=g_recv, device_id=(dp, me), device_id_type=MESH,
    ).wait_send()


def shards(grad_out, route_prob, expert_ids, saved_act, down_weight):
    vmem = pl.BlockSpec(memory_space=pltpu.VMEM)
    anywhere = pl.BlockSpec(memory_space=pl.ANY)
    dma = pltpu.SemaphoreType.DMA
    act, grad_weight, grad_prob = pl.pallas_call(
        kernel,
        out_shape=[
            jax.ShapeDtypeStruct((SLOTS, FFW), BF16),
            jax.ShapeDtypeStruct((128, FFW), F32),
            jax.ShapeDtypeStruct((1, TOK), F32),
        ],
        in_specs=[vmem, vmem, anywhere, anywhere, anywhere],
        out_specs=[vmem, vmem, vmem],
        scratch_shapes=[
            pltpu.VMEM((TOK, WIDTH), BF16),
            pltpu.VMEM((SLOTS, FFW), BF16),
            pltpu.VMEM((FFW, WIDTH), BF16),
            pltpu.VMEM((SLOTS, TOK), F32),
            pltpu.VMEM((256, 256), BF16),
            pltpu.VMEM((SLOTS, SLOTS), BF16),
            pltpu.VMEM((NE, CAP * PIECES, 128), BF16),
            pltpu.VMEM((NE, CAP * PIECES, 128), BF16),
            pltpu.VMEM((NE, 1, 128), F32),
            pltpu.VMEM((NE, 1, 128), F32),
            pltpu.VMEM((NE, 1, 128), F32),
            pltpu.VMEM((NE, 1, 128), F32),
            pltpu.VMEM((SLOTS, WIDTH), BF16),
            pltpu.VMEM((SLOTS, FFW), BF16),
            pltpu.VMEM((CHUNKS, NDP, ROWS, 128), BF16),
            pltpu.VMEM((CHUNKS, NDP, ROWS, 128), BF16),
            pltpu.VMEM((CHUNKS, NDP, ROWS, FFW), BF16),
            dma((3,)),
            dma, dma((CHUNKS,)),
            dma, dma((CHUNKS,)),
            dma, dma,
            dma, dma((CHUNKS,)),
            dma, dma((4, CHUNKS)), dma((4, CHUNKS)), dma,
        ],
        compiler_params=pltpu.CompilerParams(
            collective_id=0, has_side_effects=True, vmem_limit_bytes=40 << 20
        ),
        cost_estimate=pl.CostEstimate(
            flops=2_000_000_000, bytes_accessed=6_000_000, transcendentals=0
        ),
    )(
        expert_ids.reshape(1, TOK), route_prob.reshape(1, TOK), grad_out,
        saved_act.reshape(SLOTS, FFW), down_weight.reshape(FFW, WIDTH),
    )
    return act[None, None], grad_weight[None], grad_prob.reshape(TOK, 1)


def solution(mesh):
    return jax.shard_map(
        shards,
        mesh=mesh,
        in_specs=(
            P(("dp", "expert"), None),
            P(("dp", "expert"), None),
            P(("dp", "expert"), None),
            P("dp", "expert", None, None),
            P("expert", None, None),
        ),
        out_specs=(
            P("dp", "expert", None, None),
            P("expert", "dp", None),
            P(("dp", "expert"), None),
        ),
        check_vma=False,
    )
```

```python
import functools

import jax
import jax.numpy as jnp
from jax import lax
from jax.experimental import pallas as pl
from jax.experimental.pallas import tpu as pltpu
from jax.sharding import PartitionSpec as P

MESH = pl.DeviceIdType.MESH
NZ, NX = 16, 4
NE = NZ * NX
NDP = 16
CAP = 3
CHUNKS = 4
PEERS = NE // CHUNKS
ROWS = PEERS * CAP
SLOTS = NE * CAP
SELF = 2 * NX
TOK = 128
WIDTH = 2048
FFW = 768
PIECES = WIDTH // 128
F32 = jnp.float32
BF16 = jnp.bfloat16


def offset_of(o):
    q = o // NX
    j, r = q // 4, q % 4
    base = jnp.where(r < 2, NZ // 2, jnp.where(r == 3, NZ, 0))
    dz = base + jnp.where((r == 1) | (r == 2), j, -j)
    return dz - jnp.where((j == 0) & (r % 2 == 1), NZ // 4, 0), o % NX


def target_of(o, z, x):
    dz, dx = offset_of(o)
    return ((z + dz) % NZ) * NX + (x + dx) % NX


def source_of(o, z, x):
    dz, dx = offset_of(o)
    return ((z + NZ - dz) % NZ) * NX + (x + NX - dx) % NX


def slot_parts(slot):
    chunk = (
        (slot >= ROWS).astype(jnp.int32)
        + (slot >= 2 * ROWS).astype(jnp.int32)
        + (slot >= 3 * ROWS).astype(jnp.int32)
    )
    rest = slot - ROWS * chunk
    return PEERS * chunk + rest % PEERS, rest // PEERS


def dot(a, b):
    return lax.dot_general(a, b, (((1,), (0,)), ((), ())), preferred_element_type=F32)


def kernel(
    ids_hbm, prob_hbm, grad_hbm, saved_hbm, weight_hbm,
    act_ref, gw_ref, gp_ref,
    ids_ref, prob_ref, grad, saved, weight, onehot, swap, to_natural,
    send, recv, psend, precv, gsend, grecv,
    arrived, act, wsend, wrecv, gathered,
    load_sem, tok_send, tok_recv, p_send, p_recv, g_send, g_recv,
    w_send, w_recv, s_send, right_recv, left_recv, twin_recv,
):
    dp, me = lax.axis_index("dp"), lax.axis_index("expert")
    z, x = me // NX, me % NX
    y, core = dp // 2, dp % 2
    twin = dp + 1 - 2 * core
    right, left = (dp + 2) % NDP, (dp + NDP - 2) % NDP

    loads = [
        pltpu.make_async_copy(ids_hbm, ids_ref, load_sem.at[3]),
        pltpu.make_async_copy(prob_hbm, prob_ref, load_sem.at[4]),
        pltpu.make_async_copy(grad_hbm, grad, load_sem.at[0]),
        pltpu.make_async_copy(saved_hbm, saved, load_sem.at[1]),
        pltpu.make_async_copy(weight_hbm, weight, load_sem.at[2]),
    ]
    for load in loads:
        load.start()

    barrier = pltpu.get_barrier_semaphore()

    for dz in (8, 7, 9, 6, 10, 5, 11, 4, 12, 3, 13, 2, 14, 1, 15, 0):
        for dx in range(NX):
            if dz or dx:
                pl.semaphore_signal(
                    barrier, inc=1, device_id=(dp, ((z + dz) % NZ) * NX + (x + dx) % NX),
                    device_id_type=MESH,
                )
    for i in range(1, NDP):
        pl.semaphore_signal(
            barrier, inc=1, device_id=((dp + i) % NDP, me), device_id_type=MESH
        )

    loads[0].wait()
    loads[1].wait()

    ids = jnp.broadcast_to(ids_ref[...], (TOK, TOK)).astype(F32)
    earlier = lax.broadcasted_iota(jnp.int32, (TOK, TOK), 0) < lax.broadcasted_iota(
        jnp.int32, (TOK, TOK), 1
    )
    same = jnp.where(earlier & (ids.T == ids), 1.0, 0.0)
    before = jnp.sum(same, axis=0, keepdims=True)
    peer, k = slot_parts(lax.broadcasted_iota(jnp.int32, (SLOTS, TOK), 0))
    onehot[...] = jnp.where(
        (target_of(peer, z, x) == ids_ref[...]) & (k.astype(F32) == before), 1.0, 0.0
    )
    lane = lax.broadcasted_iota(jnp.int32, (PEERS, 128), 1)

    def by_lane(column):
        out = jnp.zeros((PEERS, 128), F32)
        for i in range(CAP):
            out = jnp.where(lane == i, column[PEERS * i : PEERS * (i + 1)], out)
        return out

    probs = jnp.sum(onehot[...] * prob_ref[...].astype(F32), axis=1, keepdims=True)
    for j in range(CHUNKS):
        psend[PEERS * j : PEERS * (j + 1), 0, :] = by_lane(probs[ROWS * j : ROWS * (j + 1)])

    row = lax.broadcasted_iota(jnp.int32, (256, 256), 0)
    col = lax.broadcasted_iota(jnp.int32, (256, 256), 1)
    swap[...] = jnp.where(col == 16 * (row % 16) + row // 16, 1.0, 0.0).astype(BF16)

    slot_r = lax.broadcasted_iota(jnp.int32, (SLOTS, SLOTS), 0)
    slot_c = lax.broadcasted_iota(jnp.int32, (SLOTS, SLOTS), 1)
    peer_r, k_r = slot_parts(slot_r)
    to_chunk = jnp.where(source_of(peer_r, z, x) * CAP + k_r == slot_c, 1.0, 0.0).astype(BF16)
    peer_c, k_c = slot_parts(slot_c)
    to_natural[...] = jnp.where(
        source_of(peer_c, z, x) * CAP + k_c == slot_r, 1.0, 0.0
    ).astype(BF16)
    loads[3].wait()
    own = dot(to_chunk, saved[...]).astype(BF16)
    for j in range(CHUNKS):
        gathered[j, dp] = own[ROWS * j : ROWS * (j + 1)]

    def pass_on(j, r, device, sem):
        pltpu.make_async_remote_copy(
            src_ref=gathered.at[j, r], dst_ref=gathered.at[j, r],
            send_sem=s_send, recv_sem=sem,
            device_id=(device, me), device_id_type=MESH,
        ).start()

    def await_piece(j, r, sem):
        pltpu.make_async_remote_copy(
            src_ref=gathered.at[j, r], dst_ref=gathered.at[j, r],
            send_sem=s_send, recv_sem=sem,
            device_id=(twin, me), device_id_type=MESH,
        ).wait_recv()

    loads[2].wait()
    for j in range(CHUNKS):
        picked = dot(onehot[ROWS * j : ROWS * (j + 1), :].astype(BF16), grad[...]).astype(BF16)
        for i in range(CAP):
            tiles = jnp.concatenate(
                [picked[PEERS * i : PEERS * (i + 1), 128 * c : 128 * (c + 1)] for c in range(PIECES)],
                axis=0,
            )
            out = dot(swap[...], tiles).astype(BF16).reshape(PEERS, PIECES, 128)
            send[PEERS * j : PEERS * (j + 1), PIECES * i : PIECES * (i + 1), :] = out
        if j == 0:
            pl.semaphore_wait(barrier, NE - 1 + NDP - 1)

        @pl.loop(PEERS * j, min(PEERS * (j + 1), NE))
        def _(o):
            @pl.when(o != SELF)
            def _():
                peer_id = (dp, target_of(o, z, x))
                pltpu.make_async_remote_copy(
                    src_ref=send.at[o], dst_ref=recv.at[o],
                    send_sem=tok_send, recv_sem=tok_recv.at[j],
                    device_id=peer_id, device_id_type=MESH,
                ).start()
                pltpu.make_async_remote_copy(
                    src_ref=psend.at[o], dst_ref=precv.at[o],
                    send_sem=p_send, recv_sem=p_recv.at[j],
                    device_id=peer_id, device_id_type=MESH,
                ).start()

        if j == 0:
            for i in range(CHUNKS):
                pass_on(i, dp, right, right_recv.at[0, i])
                pass_on(i, dp, left, left_recv.at[0, i])
            for i in range(CHUNKS):
                pass_on(i, dp, twin, twin_recv)
    recv[SELF] = send[SELF]
    precv[SELF] = psend[SELF]

    for hop in range(1, 5):
        from_left, from_right = (dp + NDP - 2 * hop) % NDP, (dp + 2 * hop) % NDP
        for j in range(CHUNKS):
            if hop < 4 or j < 2:
                await_piece(j, from_left, right_recv.at[hop - 1, j])
                if hop < 3 or (hop == 3 and j < 2):
                    pass_on(j, from_left, right, right_recv.at[hop, j])
                pass_on(j, from_left, twin, twin_recv)
            if hop < 4 or j >= 2:
                await_piece(j, from_right, left_recv.at[hop - 1, j])
                if hop < 3 or (hop == 3 and j >= 2):
                    pass_on(j, from_right, left, left_recv.at[hop, j])
                pass_on(j, from_right, twin, twin_recv)
    loads[4].wait()

    def take(j):
        count = PEERS - (1 if j == SELF // PEERS else 0)
        pltpu.make_async_remote_copy(
            src_ref=send.at[pl.ds(0, count)], dst_ref=recv.at[pl.ds(0, count)],
            send_sem=tok_send, recv_sem=tok_recv.at[j],
            device_id=(dp, me), device_id_type=MESH,
        ).wait_recv()
        pltpu.make_async_remote_copy(
            src_ref=psend.at[pl.ds(0, count)], dst_ref=precv.at[pl.ds(0, count)],
            send_sem=p_send, recv_sem=p_recv.at[j],
            device_id=(dp, me), device_id_type=MESH,
        ).wait_recv()
        factor = precv[PEERS * j : PEERS * (j + 1), 0, :]
        for i in range(CAP):
            tiles = recv[PEERS * j : PEERS * (j + 1), PIECES * i : PIECES * (i + 1), :]
            turned = dot(swap[...], tiles.reshape(PEERS * PIECES, 128))
            part = jnp.broadcast_to(factor[:, i : i + 1], (PEERS, 128))
            at = ROWS * j + PEERS * i
            for c in range(PIECES):
                tile = turned[PEERS * c : PEERS * (c + 1)]
                arrived[at : at + PEERS, 128 * c : 128 * (c + 1)] = tile.astype(BF16)
                wsend[j, c, PEERS * i : PEERS * (i + 1), :] = (tile * part).astype(BF16)
        wrecv[j, dp] = wsend[j, dp]

        @pl.loop(1, NDP)
        def _(i):
            to = (dp + i) % NDP
            pltpu.make_async_remote_copy(
                src_ref=wsend.at[j, to], dst_ref=wrecv.at[j, dp],
                send_sem=w_send, recv_sem=w_recv.at[j],
                device_id=(to, me), device_id_type=MESH,
            ).start()

    def back(j):
        rows = slice(ROWS * j, ROWS * (j + 1))
        backed = lax.dot_general(
            arrived[rows, :], weight[...], (((1,), (1,)), ((), ())), preferred_element_type=F32
        )
        mine = gathered[j, dp].astype(F32)
        gsend[PEERS * j : PEERS * (j + 1), 0, :] = by_lane(
            jnp.sum(backed * mine, axis=1, keepdims=True)
        )

        @pl.loop(PEERS * j, PEERS * (j + 1))
        def _(o):
            @pl.when(o != SELF)
            def _():
                pltpu.make_async_remote_copy(
                    src_ref=gsend.at[o], dst_ref=grecv.at[o],
                    send_sem=g_send, recv_sem=g_recv,
                    device_id=(dp, source_of(o, z, x)), device_id_type=MESH,
                ).start()

        factor = precv[PEERS * j : PEERS * (j + 1), 0, :]
        for i in range(CAP):
            part = jnp.broadcast_to(factor[:, i : i + 1], (PEERS, FFW))
            at = PEERS * i
            act[ROWS * j + at : ROWS * j + at + PEERS, :] = (
                part * backed[at : at + PEERS]
            ).astype(BF16)

    def add(j):
        pltpu.make_async_remote_copy(
            src_ref=wsend.at[j, pl.ds(0, NDP - 1)], dst_ref=wrecv.at[j, pl.ds(0, NDP - 1)],
            send_sem=w_send, recv_sem=w_recv.at[j],
            device_id=(dp, me), device_id_type=MESH,
        ).wait_recv()
        part = lax.dot_general(
            wrecv[j].reshape(NDP * ROWS, 128), gathered[j].reshape(NDP * ROWS, FFW),
            (((0,), (0,)), ((), ())), preferred_element_type=F32,
        )
        if j == 0:
            gw_ref[...] = part
        else:
            gw_ref[...] += part

    take(0)
    back(0)
    take(1)
    back(1)
    pltpu.make_async_remote_copy(
        src_ref=gathered.at[:, pl.ds(0, NDP // 2)], dst_ref=gathered.at[:, pl.ds(0, NDP // 2)],
        send_sem=s_send, recv_sem=twin_recv, device_id=(twin, me), device_id_type=MESH,
    ).wait_recv()
    take(2)
    back(2)
    add(0)
    take(3)
    back(3)
    grecv[SELF] = gsend[SELF]
    add(1)
    add(2)
    act_ref[...] = dot(to_natural[...], act[...]).astype(BF16)
    add(3)

    def all_but_one(ref, sem):
        return pltpu.make_async_remote_copy(
            src_ref=ref.at[pl.ds(0, NE - 1)], dst_ref=ref.at[pl.ds(0, NE - 1)],
            send_sem=sem, recv_sem=g_recv, device_id=(dp, me), device_id_type=MESH,
        )

    all_but_one(grecv, g_send).wait_recv()
    total = jnp.zeros((PEERS, TOK), F32)
    for j in range(CHUNKS):
        back_sum = grecv[PEERS * j : PEERS * (j + 1), 0, :]
        for i in range(CAP):
            at = ROWS * j + PEERS * i
            total += onehot[at : at + PEERS, :] * jnp.broadcast_to(
                back_sum[:, i : i + 1], (PEERS, TOK)
            )
    gp_ref[...] = jnp.sum(total, axis=0, keepdims=True)

    all_but_one(send, tok_send).wait_send()
    all_but_one(psend, p_send).wait_send()
    all_but_one(gsend, g_send).wait_send()
    pltpu.make_async_remote_copy(
        src_ref=wsend.at[:, pl.ds(0, NDP - 1)], dst_ref=wsend.at[:, pl.ds(0, NDP - 1)],
        send_sem=w_send, recv_sem=g_recv, device_id=(dp, me), device_id_type=MESH,
    ).wait_send()
    pltpu.make_async_remote_copy(
        src_ref=gathered.at[:, pl.ds(0, NDP - 1)], dst_ref=gathered.at[:, pl.ds(0, NDP - 1)],
        send_sem=s_send, recv_sem=g_recv, device_id=(dp, me), device_id_type=MESH,
    ).wait_send()


def shards(grad_out, route_prob, expert_ids, saved_act, down_weight):
    vmem = pl.BlockSpec(memory_space=pltpu.VMEM)
    hbm = pl.BlockSpec(memory_space=pltpu.HBM)
    dma = pltpu.SemaphoreType.DMA
    act, grad_weight, grad_prob = pl.pallas_call(
        kernel,
        out_shape=[
            jax.ShapeDtypeStruct((SLOTS, FFW), BF16),
            jax.ShapeDtypeStruct((128, FFW), F32),
            jax.ShapeDtypeStruct((1, TOK), F32),
        ],
        in_specs=[hbm] * 5,
        out_specs=[vmem, vmem, vmem],
        scratch_shapes=[
            pltpu.VMEM((1, TOK), jnp.int32),
            pltpu.VMEM((1, TOK), BF16),
            pltpu.VMEM((TOK, WIDTH), BF16),
            pltpu.VMEM((SLOTS, FFW), BF16),
            pltpu.VMEM((FFW, WIDTH), BF16),
            pltpu.VMEM((SLOTS, TOK), F32),
            pltpu.VMEM((256, 256), BF16),
            pltpu.VMEM((SLOTS, SLOTS), BF16),
            pltpu.VMEM((NE, CAP * PIECES, 128), BF16),
            pltpu.VMEM((NE, CAP * PIECES, 128), BF16),
            pltpu.VMEM((NE, 1, 128), F32),
            pltpu.VMEM((NE, 1, 128), F32),
            pltpu.VMEM((NE, 1, 128), F32),
            pltpu.VMEM((NE, 1, 128), F32),
            pltpu.VMEM((SLOTS, WIDTH), BF16),
            pltpu.VMEM((SLOTS, FFW), BF16),
            pltpu.VMEM((CHUNKS, NDP, ROWS, 128), BF16),
            pltpu.VMEM((CHUNKS, NDP, ROWS, 128), BF16),
            pltpu.VMEM((CHUNKS, NDP, ROWS, FFW), BF16),
            dma((5,)),
            dma, dma((CHUNKS,)),
            dma, dma((CHUNKS,)),
            dma, dma,
            dma, dma((CHUNKS,)),
            dma, dma((4, CHUNKS)), dma((4, CHUNKS)), dma,
        ],
        compiler_params=pltpu.CompilerParams(
            collective_id=0, has_side_effects=True, vmem_limit_bytes=60 << 20
        ),
        cost_estimate=pl.CostEstimate(
            flops=2_000_000_000, bytes_accessed=6_000_000, transcendentals=0
        ),
    )(
        expert_ids.reshape(1, TOK), route_prob.reshape(1, TOK), grad_out,
        saved_act.reshape(SLOTS, FFW), down_weight.reshape(FFW, WIDTH),
    )
    return act[None, None], grad_weight[None], grad_prob.reshape(TOK, 1)


def solution(mesh):
    return jax.shard_map(
        shards,
        mesh=mesh,
        in_specs=(
            P(("dp", "expert"), None),
            P(("dp", "expert"), None),
            P(("dp", "expert"), None),
            P("dp", "expert", None, None),
            P("expert", None, None),
        ),
        out_specs=(
            P("dp", "expert", None, None),
            P("expert", "dp", None),
            P(("dp", "expert"), None),
        ),
        check_vma=False,
    )
```
